256 devices in a mesh: band: 64 (over z, y, x_hi), grid: 4 (over x_lo, core).
Axes of the slice: x: 4 (x_hi: 2, x_lo: 2; x = x_hi * 2 + x_lo), y: 4, z: 8, core: 2. Of those that a mesh axis runs over, the one named last changes fastest.
Arguments:
- orbitals: float32 [64, 64, 4096], P('band', 'grid')
- counts: int32 [64], P('band'), may hold values from 1 to 3, 144 in all
- partners: int32 [64, 3], P('band'), may hold values from 0 to 63, as said below
Outputs:
- applied: float32 [64, 64, 4096], P('band', 'grid')
The draws below stay inside these ranges and needn't reach their ends.
Inputs may be any that keep to these rules, and one draw needn't show every extreme that they name: `counts`: some band has exactly 3 listed partners. `partners`: for band i held by band device m = i, every entry j (used or not) satisfies 0 < (j - i) mod 64 and (j - m) mod 64 < 4; the entries of one band are distinct.
All inputs are finite; a program needn't handle non-finite values. No bound on the sum of `counts` on one device may be relied on, other than what follows from the above.
Results may differ from the reference program's by a relative error of at most 0.0001.
Values sent between devices are 32-bit elements; how exact they have to be, the bound alone decides.
A program may use at most 64 MiB of HBM per device.

```python
import math
import jax
import jax.numpy as jnp
import numpy as np
from jax import lax

NG = 64
BAND_DEV = 1
BANDS = 64
WIN = 4
K = 3


def draw_orbitals(key, part):
    key = jax.random.fold_in(key, 5)
    first = jax.random.fold_in(key, 0)
    return (0.25 * jax.random.normal(first, (BANDS, NG, NG * NG), jnp.float32)).astype(jnp.float32)


def draw_partners(key, part):
    key = jax.random.fold_in(key, 11)
    span = WIN * BAND_DEV - 1
    slots = jnp.arange(BANDS, dtype=jnp.int32)[:, None]
    within = slots % BAND_DEV
    steps_ahead = jnp.arange(1, span + 1, dtype=jnp.int32)[None, :]
    scores = jax.random.randint(key, (BANDS, span), 0, 1 << 20, dtype=jnp.int32) * 256 + steps_ahead
    scores = jnp.where(steps_ahead <= span - within, scores, -1)
    _, picked = lax.top_k(scores, K)
    return ((slots + picked.astype(jnp.int32) + 1) % BANDS).astype(jnp.int32)


def profile(number_of, total, reach, skew):
    portions = [(1 << 20) // math.isqrt(grade ** skew) + 1 for grade in range(2, number_of + 1)]
    spare, given = total - reach - (number_of - 1), [1] * (number_of - 1)
    while spare > 0:
        movable = [i for i in range(number_of - 1) if given[i] < reach]
        mass, budget = sum([portions[i] for i in movable]), spare
        for i in movable:
            more = min(reach - given[i], max(1, budget * portions[i] // mass), spare)
            given[i] = given[i] + more
            spare = spare - more
    return np.array([reach] + given)


def uneven_parts(own_key, amount, total, reach, slope):
    if amount == 2:
        one = jax.random.randint(own_key, (), max(1, total - reach), min(reach, total - 1) + 1)
        return jnp.stack([one, total - one])
    tallies = jnp.asarray(profile(amount, total, reach, slope), jnp.int32)
    couples = (amount - 1) // 2
    donor, taker = tallies[1:1 + 2 * couples:2], tallies[2:2 + 2 * couples:2]
    room = jnp.minimum(donor - 1, reach - taker)
    passed = jax.random.randint(jax.random.fold_in(own_key, 1), (couples,), 0, 1 << 20) % (room + 1)
    tallies = tallies.at[1:1 + 2 * couples:2].set(donor - passed).at[2:2 + 2 * couples:2].set(taker + passed)
    return tallies[jax.random.permutation(jax.random.fold_in(own_key, 2), amount)]


def setup_inputs(seed: int = 0) -> dict:
    keys = jax.random.split(jax.random.key(seed), 4)
    return {
        "orbitals": draw_orbitals(jax.random.fold_in(keys[3], 71), 0),
        "counts": uneven_parts(keys[1], BANDS, BANDS * K * 3 // 4, K, 2).astype(jnp.int32),
        "partners": draw_partners(jax.random.fold_in(keys[3], 71), 0),
    }


def coulomb_table():
    freq = (jnp.fft.fftfreq(NG) * (2.0 * math.pi)).astype(jnp.float32)
    total_sq = freq[:, None, None] ** 2 + freq[None, :, None] ** 2 + freq[None, None, :] ** 2
    safe = jnp.where(total_sq > 0, total_sq, jnp.float32(1.0))
    return jnp.where(total_sq > 0, 4.0 * math.pi / safe, 0.0).astype(jnp.float32)


def reference(orbitals, counts, partners):
    cubes = orbitals.reshape(BANDS, NG, NG, NG)
    coulomb = coulomb_table()
    alive = (jnp.arange(K, dtype=jnp.int32)[None, :] < counts[:, None]).astype(jnp.float32)

    def one_band(carry, item):
        field, partner_ids, alive_row = item
        partner_rows = cubes[partner_ids]
        density = field[None] * partner_rows * alive_row[:, None, None, None]
        spectrum = jnp.fft.fftn(density, axes=(1, 2, 3)) * coulomb
        potential = jnp.real(jnp.fft.ifftn(spectrum, axes=(1, 2, 3))).astype(jnp.float32)
        own_term = jnp.sum(potential * partner_rows, axis=0)
        carry = carry.at[partner_ids].add(potential * field[None])
        return carry, own_term

    start = jnp.zeros((BANDS, NG, NG, NG), jnp.float32)
    pushed, own_terms = lax.scan(one_band, start, (cubes, partners, alive))
    return (pushed + own_terms).reshape(BANDS, NG, NG * NG)
```

```python
import functools
import math

import jax
import jax.numpy as jnp
import ml_dtypes
import numpy as np
from jax import lax
from jax.experimental import pallas as pl
from jax.experimental.pallas import tpu as pltpu
from jax.sharding import PartitionSpec as P

MESH = pl.DeviceIdType.MESH
F32, BF16 = jnp.float32, jnp.bfloat16
NG = 64
PLANE = NG * NG
WIDE = PLANE + 128
A, B, C, D, E = range(5)
PAIRS = ((B, C, 1), (B, D, 2), (C, D, 1), (A, D, 3), (B, E, 3), (C, E, 2))
PER = 2
CHUNKS = len(PAIRS) // PER


def basis():
    n = np.arange(NG)
    rows = [np.full(NG, 1 / 8)]
    rows += [np.cos(2 * np.pi * k * n / NG) * math.sqrt(2) / 8 for k in range(1, 32)]
    rows += [np.cos(np.pi * n) / 8]
    rows += [np.sin(2 * np.pi * k * n / NG) * math.sqrt(2) / 8 for k in range(1, 32)]
    return np.stack(rows)


def halves(m):
    high = m.astype(np.float32).astype(ml_dtypes.bfloat16)
    low = (m - high.astype(np.float64)).astype(np.float32).astype(ml_dtypes.bfloat16)
    return high, low


def left(m):
    high, low = halves(m)
    return np.concatenate([high, high, low], 1)


def right(m):
    high, low = halves(m)
    return np.concatenate([np.concatenate([high, low], 1), np.concatenate([high, np.zeros_like(low)], 1)], 0)


def tables():
    r = basis()
    zero = np.zeros_like(r)
    z_fwd = np.block([[r.T, zero], [zero, r.T]])
    z_inv = np.block([[r, zero], [zero, r]])
    t = {(e, q): r[32 * e : 32 * e + 32, q::2] for e in range(2) for q in range(2)}
    y_fwd = np.block([[t[0, 0], t[0, 1]], [t[1, 1], t[1, 0]]])
    y_inv = np.block([[t[0, 0].T, t[1, 0].T], [t[1, 1].T, t[0, 1].T]])
    return (
        np.stack([right(z_fwd), right(z_inv)]),
        np.stack([left(y_fwd), left(y_inv), left(r), left(r.T)]),
    )


def split(x):
    high = x.astype(BF16)
    return high, (x - high.astype(F32)).astype(BF16)


def dot(a, b):
    return lax.dot_general(a, b, (((1,), (0,)), ((), ())), preferred_element_type=F32)


def from_left(matrix, x):
    high, low = split(x)
    return dot(matrix, jnp.concatenate([high, low, high], 0))


def from_right(x, matrix):
    high, low = split(x)
    both = dot(jnp.concatenate([high, low], 1), matrix)
    return both[:, :128] + both[:, 128:]


def along_y(ref, field, matrix):
    parts = []
    for f in range(PER):
        for x in range(8):
            parts.append(ref[field + f, pl.ds(x, 32, stride=8), :])
    both = jnp.concatenate(parts, 1)
    other = jnp.concatenate([jnp.concatenate([v[:, 64:], v[:, :64]], 1) for v in parts], 1)
    out = from_left(matrix, jnp.concatenate([both, other], 0))
    lane = lax.broadcasted_iota(jnp.int32, (32, 128), 1)
    res = []
    for n in range(8 * PER):
        piece = out[:, 128 * n : 128 * (n + 1)]
        res.append(jnp.where(lane < 64, piece[:32], piece[32:]))
    return res


def freq_sq(index):
    f = jnp.where(index <= 32, index, index - 32).astype(F32) * F32(2 * math.pi / NG)
    return f * f


def kernel(
    orb, counts, partners, wz_ref, wl_ref, out_ref,
    band, other, s1, s2, got, back, s3, s4, acc, ret, lam,
    local_sem, f_send, f_recv, t1_send, t1_recv, t2_send, t2_recv, r_send, r_recv,
):
    m = lax.axis_index("band")
    g = lax.axis_index("grid")
    p, h = m // 2, m % 2
    me = 2 * g + h
    n_bands = 64

    def at(dp, hh):
        return ((2 * p + 2 * dp + n_bands) % n_bands + hh, g)

    def peer(slot):
        return (2 * p + slot % 2, slot // 2)

    def remote(src, dst, send, recv, device):
        return pltpu.make_async_remote_copy(
            src_ref=src, dst_ref=dst, send_sem=send, recv_sem=recv, device_id=device, device_id_type=MESH
        )

    own = pltpu.make_async_copy(orb.at[pl.ds(8 * h, 8), :], band.at[1 + h, :, pl.ds(0, PLANE)], local_sem.at[0])
    rest = pltpu.make_async_copy(orb.at[pl.ds(8 * (1 - h), 8), :], other.at[:, pl.ds(0, PLANE)], local_sem.at[1])
    own.start()
    rest.start()

    barrier = pltpu.get_barrier_semaphore()
    for k in range(1, 8):
        pl.semaphore_signal(barrier, inc=1, device_id=peer(me ^ k), device_id_type=MESH)
    for dp in (-1, 1):
        for hh in range(2):
            pl.semaphore_signal(barrier, inc=1, device_id=at(dp, hh), device_id_type=MESH)

    row = lax.broadcasted_iota(jnp.int32, (8, 128), 0)
    tile = jnp.zeros((8, 128), F32)
    for d in range(1, 4):
        listed = jnp.float32(0.0)
        for k in range(3):
            hit = ((partners[0, k] - m + n_bands) % n_bands == d) & (counts[0] > k)
            listed = listed + jnp.where(hit, jnp.float32(1.0), jnp.float32(0.0))
        tile = jnp.where(row == d - 1, listed, tile)
    band[1 + h, :, PLANE:] = tile
    other[:, PLANE:] = tile

    kx = freq_sq(lax.broadcasted_iota(jnp.int32, (NG, 128), 0))
    lane = lax.broadcasted_iota(jnp.int32, (NG, 128), 1)
    kz = freq_sq(lane % 64)
    for i in range(4):
        ky = freq_sq(4 * me + i + jnp.where(lane < 64, 0, 32))
        total = kx + ky + kz
        some = total > 0
        lam[:, 128 * i : 128 * (i + 1)] = jnp.where(some, F32(4 * math.pi) / jnp.where(some, total, 1.0), 0.0)

    own.wait()
    rest.wait()
    pl.semaphore_wait(barrier, 11)

    mine = band.at[1 + h]
    fetches = [
        remote(other, band.at[1 + h], f_send.at[0], f_recv.at[1 + h], at(0, 1 - h)),
        remote(other, band.at[3 + h], f_send.at[1], f_recv.at[3 + h], at(-1, 1 - h)),
        remote(mine, band.at[3 + h], f_send.at[2], f_recv.at[3 + h], at(-1, h)),
    ]
    upward = [
        remote(other, band.at[A], f_send.at[3], f_recv.at[A], at(1, 0)),
        remote(mine, band.at[A], f_send.at[4], f_recv.at[A], at(1, 1)),
    ]
    for copy in fetches:
        copy.start()

    @pl.when(h == 1)
    def _():
        for copy in upward:
            copy.start()

    def fetched(slot):
        remote(other, band.at[slot], f_send.at[0], f_recv.at[slot], at(0, 0)).wait_recv()

    fetched(2 - h)
    ready = {B, C}
    sent1 = []
    order = (1, 3, 5, 7, 4, 6, 2)
    for c in range(CHUNKS):
        f0 = PER * c
        for f in range(f0, f0 + PER):
            low, high, d = PAIRS[f]
            for slot in (low, high):
                if slot not in ready:
                    fetched(slot)
                    ready.add(slot)
            alive = jnp.broadcast_to(band[low, d - 1 : d, PLANE:], (8, 128))
            pieces = []
            for j in range(32):
                cut = slice(128 * j, 128 * (j + 1))
                pieces.append(band[low, :, cut] * band[high, :, cut] * alive)
            s1[f] = from_right(jnp.concatenate(pieces, 0), wz_ref[0])
        res = along_y(s1, f0, wl_ref[0])
        for f in range(PER):
            for x in range(8):
                s2[f0 + f, pl.ds(x, 32, stride=8), :] = res[8 * f + x]
        for k in order:
            to = me ^ k
            copy = remote(
                s2.at[pl.ds(f0, PER), pl.ds(pl.multiple_of(32 * to, 32), 32)],
                got.at[me, pl.ds(f0, PER)],
                t1_send.at[c, k], t1_recv.at[c, k], peer(to),
            )
            copy.start()
            sent1.append(copy)
        got[me, f0 : f0 + PER] = s2[f0 : f0 + PER, pl.ds(pl.multiple_of(32 * me, 32), 32)]

    sent2 = []
    for c in range(CHUNKS):
        f0 = PER * c
        for k in order:
            remote(
                s2.at[pl.ds(f0, PER), pl.ds(0, 32)], got.at[me ^ k, pl.ds(f0, PER)],
                t1_send.at[c, k], t1_recv.at[c, k], peer(me ^ k),
            ).wait_recv()
        columns = []
        for f in range(f0, f0 + PER):
            for i in range(4):
                columns.append(jnp.concatenate([got[s, f, 8 * i : 8 * i + 8, :] for s in range(8)], 0))
        wave = from_left(wl_ref[2], jnp.concatenate(columns, 1))
        wave = wave * jnp.concatenate([lam[...]] * PER, 1)
        wave = from_left(wl_ref[3], wave)
        for f in range(PER):
            for i in range(4):
                n = 4 * f + i
                for s in range(8):
                    back[s, f0 + f, 8 * i : 8 * i + 8, :] = wave[8 * s : 8 * s + 8, 128 * n : 128 * (n + 1)]
        for k in order:
            to = me ^ k
            copy = remote(
                back.at[to, pl.ds(f0, PER)],
                s3.at[pl.ds(f0, PER), pl.ds(pl.multiple_of(32 * me, 32), 32)],
                t2_send.at[c, k], t2_recv.at[c, k], peer(to),
            )
            copy.start()
            sent2.append(copy)
        s3[f0 : f0 + PER, pl.ds(pl.multiple_of(32 * me, 32), 32)] = back[me, f0 : f0 + PER]

    gives = {
        D: remote(acc.at[D], ret.at[1 + h], r_send.at[0], r_recv.at[1 + h], at(1, 0)),
        A: remote(acc.at[A], ret.at[3 + h], r_send.at[1], r_recv.at[3 + h], at(-1, 1)),
        E: remote(acc.at[E], ret.at[1 + h], r_send.at[2], r_recv.at[1 + h], at(1, 1)),
        C: remote(acc.at[2 - h], ret.at[0], r_send.at[3], r_recv.at[0], at(0, 1 - h)),
    }
    begun = set()
    last = {slot: max(f for f, pair in enumerate(PAIRS) if slot in pair[:2]) for slot in range(5)}
    for c in range(CHUNKS):
        f0 = PER * c
        for k in order:
            remote(
                back.at[0, pl.ds(f0, PER)], s3.at[pl.ds(f0, PER), pl.ds(pl.multiple_of(32 * (me ^ k), 32), 32)],
                t2_send.at[c, k], t2_recv.at[c, k], peer(me ^ k),
            ).wait_recv()
        res = along_y(s3, f0, wl_ref[1])
        for f in range(PER):
            for x in range(8):
                s4[f0 + f, pl.ds(x, 32, stride=8), :] = res[8 * f + x]
        for f in range(f0, f0 + PER):
            low, high, _ = PAIRS[f]
            potential = from_right(s4[f], wz_ref[1])
            for j in range(32):
                cut = slice(128 * j, 128 * (j + 1))
                v = potential[8 * j : 8 * j + 8]
                for to, by in ((low, high), (high, low)):
                    term = v * band[by, :, cut]
                    acc[to, :, cut] = acc[to, :, cut] + term if to in begun else term
            begun |= {low, high}
        for slot, copy in gives.items():
            if f0 <= last[slot] < f0 + PER:
                copy.start()

    def returned(slot):
        remote(acc.at[0], ret.at[slot], r_send.at[0], r_recv.at[slot], at(0, 0)).wait_recv()

    returned(1)
    returned(2)

    @pl.when(h == 1)
    def _():
        returned(3)
        returned(4)
        ret[1] = ret[1] + ret[3]
        ret[2] = ret[2] + ret[4]

    out_ref[pl.ds(pl.multiple_of(8 * h, 8), 8), :] = acc[1 + h] + ret[1 + h]
    returned(0)
    out_ref[pl.ds(pl.multiple_of(8 * (1 - h), 8), 8), :] = ret[0] + ret[2 - h]

    for copy in fetches + sent1 + sent2 + list(gives.values()):
        copy.wait_send()

    @pl.when(h == 1)
    def _():
        for copy in upward:
            copy.wait_send()


def shards(orbitals, counts, partners):
    wz, wl = tables()
    fields = len(PAIRS)
    vmem = pl.BlockSpec(memory_space=pltpu.VMEM)
    smem = pl.BlockSpec(memory_space=pltpu.SMEM)
    dma = pltpu.SemaphoreType.DMA
    applied = pl.pallas_call(
        kernel,
        out_shape=jax.ShapeDtypeStruct((16, PLANE), F32),
        in_specs=[pl.BlockSpec(memory_space=pl.ANY), smem, smem, vmem, vmem],
        out_specs=vmem,
        scratch_shapes=[
            pltpu.VMEM((5, 8, WIDE), F32),
            pltpu.VMEM((8, WIDE), F32),
            pltpu.VMEM((fields, 256, 128), F32),
            pltpu.VMEM((fields, 256, 128), F32),
            pltpu.VMEM((8, fields, 32, 128), F32),
            pltpu.VMEM((8, fields, 32, 128), F32),
            pltpu.VMEM((fields, 256, 128), F32),
            pltpu.VMEM((fields, 256, 128), F32),
            pltpu.VMEM((5, 8, PLANE), F32),
            pltpu.VMEM((5, 8, PLANE), F32),
            pltpu.VMEM((NG, 512), F32),
            dma((2,)),
            dma((5,)),
            dma((5,)),
            dma((CHUNKS, 8)),
            dma((CHUNKS, 8)),
            dma((CHUNKS, 8)),
            dma((CHUNKS, 8)),
            dma((4,)),
            dma((5,)),
        ],
        compiler_params=pltpu.CompilerParams(
            collective_id=0, has_side_effects=True, vmem_limit_bytes=32 * 1024 * 1024
        ),
        cost_estimate=pl.CostEstimate(flops=500_000_000, bytes_accessed=1 << 20, transcendentals=0),
    )(orbitals.reshape(16, PLANE), counts, partners, jnp.asarray(wz), jnp.asarray(wl))
    return applied.reshape(1, 16, PLANE)


def solution(mesh):
    in_specs = (P("band", "grid", None), P("band"), P("band", None))
    out_specs = P("band", "grid", None)
    return jax.shard_map(shards, mesh=mesh, in_specs=in_specs, out_specs=out_specs, check_vma=False)
```

```python
import functools
import math

import jax
import jax.numpy as jnp
import ml_dtypes
import numpy as np
from jax import lax
from jax.experimental import pallas as pl
from jax.experimental.pallas import tpu as pltpu
from jax.sharding import PartitionSpec as P

MESH = pl.DeviceIdType.MESH
F32, BF16 = jnp.float32, jnp.bfloat16
NG = 64
PLANE = NG * NG
B, C, D, E, F = range(5)
PAIRS = ((D, E, 1), (C, F, 3), (C, D, 1), (C, E, 2), (B, D, 2), (B, E, 3))
RUNS = ((0, 1), (1, 2), (3, 2), (5, 1))
PLAN = (("f", 0), ("f", 1), ("f", 2), ("x", 0), ("f", 3), ("x", 1), ("x", 2), ("x", 3), ("i", 0), ("i", 1), ("i", 2), ("i", 3))


def basis():
    n = np.arange(NG)
    rows = [np.full(NG, 1 / 8)]
    rows += [np.cos(2 * np.pi * k * n / NG) * math.sqrt(2) / 8 for k in range(1, 32)]
    rows += [np.cos(np.pi * n) / 8]
    rows += [np.sin(2 * np.pi * k * n / NG) * math.sqrt(2) / 8 for k in range(1, 32)]
    return np.stack(rows)


def halves(m):
    high = m.astype(np.float32).astype(ml_dtypes.bfloat16)
    low = (m - high.astype(np.float64)).astype(np.float32).astype(ml_dtypes.bfloat16)
    return high, low


def left(m):
    high, low = halves(m)
    return np.concatenate([high, high, low], 1)


def right(m):
    high, low = halves(m)
    return np.concatenate([np.concatenate([high, low], 1), np.concatenate([high, np.zeros_like(low)], 1)], 0)


def tables():
    r = basis()
    zero = np.zeros_like(r)
    z_fwd = np.block([[r.T, zero], [zero, r.T]])
    z_inv = np.block([[r, zero], [zero, r]])
    t = {(e, q): r[32 * e : 32 * e + 32, q::2] for e in range(2) for q in range(2)}
    y_fwd = np.block([[t[0, 0], t[0, 1]], [t[1, 1], t[1, 0]]])
    y_inv = np.block([[t[0, 0].T, t[1, 0].T], [t[1, 1].T, t[0, 1].T]])
    return (
        np.stack([right(z_fwd), right(z_inv)]),
        np.stack([left(y_fwd), left(y_inv), left(r), left(r.T)]),
    )


def split(x):
    high = x.astype(BF16)
    return high, (x - high.astype(F32)).astype(BF16)


def dot(a, b):
    return lax.dot_general(a, b, (((1,), (0,)), ((), ())), preferred_element_type=F32)


def from_left(matrix, x):
    high, low = split(x)
    return dot(matrix, jnp.concatenate([high, low, high], 0))


def from_right(x, matrix):
    high, low = split(x)
    both = dot(jnp.concatenate([high, low], 1), matrix)
    return both[:, :128] + both[:, 128:]


def along_y(ref, first, count, matrix):
    parts = []
    for f in range(first, first + count):
        for x in range(8):
            parts.append(ref[f, pl.ds(x, 32, stride=8), :])
    both = jnp.concatenate(parts, 1)
    other = jnp.concatenate([jnp.concatenate([v[:, 64:], v[:, :64]], 1) for v in parts], 1)
    out = from_left(matrix, jnp.concatenate([both, other], 0))
    lane = lax.broadcasted_iota(jnp.int32, (32, 128), 1)
    res = []
    for n in range(8 * count):
        piece = out[:, 128 * n : 128 * (n + 1)]
        res.append(jnp.where(lane < 64, piece[:32], piece[32:]))
    return res


def freq_sq(index):
    f = jnp.where(index <= 32, index, index - 32).astype(F32) * F32(2 * math.pi / NG)
    return f * f


def kernel(
    orb, counts_in, partners_in, wz_in, wl_in, out_ref,
    counts, partners, wz_ref, wl_ref, band, listed, s1, s2, got, back, s3, s4, acc, ret, lam,
    local_sem, hello, f_send, f_recv, a_send, a_recv, t1_send, t1_recv, t2_send, t2_recv, r_send, r_recv,
):
    m = lax.axis_index("band")
    g = lax.axis_index("grid")
    p, h = m // 2, m % 2
    me = 2 * g + h
    n_bands = 64

    def at(dp, hh):
        return ((2 * p + 2 * dp + n_bands) % n_bands + hh, g)

    def peer(slot):
        return (2 * p + slot % 2, slot // 2)

    def remote(src, dst, send, recv, device):
        return pltpu.make_async_remote_copy(
            src_ref=src, dst_ref=dst, send_sem=send, recv_sem=recv, device_id=device, device_id_type=MESH
        )

    barrier = pltpu.get_barrier_semaphore()
    for device in [at(-1, 0), at(-1, 1)] + [peer(me ^ k) for k in (1, 2, 4, 6)]:
        pl.semaphore_signal(barrier, inc=1, device_id=device, device_id_type=MESH)

    def rows(half):
        return pl.ds(pl.multiple_of(8 * half, 8), 8)

    mine, rest = orb.at[rows(h)], orb.at[rows(1 - h)]
    local = [
        pltpu.make_async_copy(src, dst, local_sem.at[n])
        for n, (src, dst) in enumerate(
            (
                (counts_in, counts), (partners_in, partners), (mine, band.at[D + h]),
                (wz_in, wz_ref), (wl_in, wl_ref),
            )
        )
    ]
    for copy in local:
        copy.start()

    pl.semaphore_wait(barrier, 6)

    def fetch(src, slot, n, device):
        return remote(src, band.at[slot], f_send.at[n], f_recv.at[slot], device)

    def fetched(slot):
        fetch(rest, slot, 0, at(0, 1 - h)).wait_recv()

    def tell(slot, n, device):
        return remote(listed.at[D + h], listed.at[slot], a_send.at[n], a_recv.at[slot], device)

    sent = [
        fetch(rest, D + h, 0, at(0, 1 - h)),
        fetch(mine, B + h, 1, at(1, h)),
    ]
    for copy in sent:
        copy.start()
    for hh in range(2):
        pl.semaphore_signal(hello, inc=1, device_id=at(1, hh), device_id_type=MESH)

    local[0].wait()
    local[1].wait()
    row = lax.broadcasted_iota(jnp.int32, (8, 128), 0)
    tile = jnp.zeros((8, 128), F32)
    for d in range(1, 4):
        weight = jnp.float32(0.0)
        for k in range(3):
            hit = ((partners[0, k] - m + n_bands) % n_bands == d) & (counts[0] > k)
            weight = weight + jnp.where(hit, jnp.float32(1.0), jnp.float32(0.0))
        tile = jnp.where(row == d - 1, weight, tile)
    listed[D + h] = tile
    told = [tell(D + h, 0, at(0, 1 - h)), tell(B + h, 1, at(1, h))]
    for copy in told:
        copy.start()
    sent += told

    kx = freq_sq(lax.broadcasted_iota(jnp.int32, (NG, 128), 0))
    lane = lax.broadcasted_iota(jnp.int32, (NG, 128), 1)
    kz = freq_sq(lane % 64)
    for i in range(4):
        ky = freq_sq(4 * me + i + jnp.where(lane < 64, 0, 32))
        total = kx + ky + kz
        some = total > 0
        lam[:, 128 * i : 128 * (i + 1)] = jnp.where(some, F32(4 * math.pi) / jnp.where(some, total, 1.0), 0.0)

    for copy in local[2:]:
        copy.wait()
    fetched(E - h)
    tell(E - h, 0, at(0, 1 - h)).wait_recv()
    on = [
        fetch(band.at[E - h], C - h, 2, at(1, h)),
        remote(listed.at[E - h], listed.at[C - h], a_send.at[2], a_recv.at[C - h], at(1, h)),
        fetch(band.at[D], F, 3, at(-1, h)),
    ]
    on[0].start()
    on[1].start()
    pl.semaphore_wait(hello, 2)
    on[2].start()
    sent += on
    ready = {D, E}
    order = (1, 3, 5, 7, 4, 6, 2)
    mine_32 = pl.ds(pl.multiple_of(32 * me, 32), 32)

    def forward(c):
        f0, count = RUNS[c]
        run = pl.ds(f0, count)
        for f in range(f0, f0 + count):
            low, high, d = PAIRS[f]
            for slot in (low, high):
                if slot not in ready:
                    fetched(slot)
                    if slot != F:
                        tell(slot, 0, at(0, 1 - h)).wait_recv()
                    ready.add(slot)
            alive = jnp.broadcast_to(listed[low, d - 1 : d, :], (8, 128))
            pieces = []
            for j in range(32):
                cut = slice(128 * j, 128 * (j + 1))
                pieces.append(band[low, :, cut] * band[high, :, cut] * alive)
            s1[f] = from_right(jnp.concatenate(pieces, 0), wz_ref[0])
        res = along_y(s1, f0, count, wl_ref[0])
        for n, piece in enumerate(res):
            s2[f0 + n // 8, pl.ds(n % 8, 32, stride=8), :] = piece
        for k in order:
            to = me ^ k
            copy = remote(
                s2.at[run, pl.ds(pl.multiple_of(32 * to, 32), 32)], got.at[me, run],
                t1_send.at[c, k], t1_recv.at[c, k], peer(to),
            )
            copy.start()
            sent.append(copy)
        got[me, f0 : f0 + count] = s2[f0 : f0 + count, mine_32]

    def across(c):
        f0, count = RUNS[c]
        run = pl.ds(f0, count)
        for k in order:
            remote(
                s2.at[run, pl.ds(0, 32)], got.at[me ^ k, run], t1_send.at[c, k], t1_recv.at[c, k], peer(me ^ k)
            ).wait_recv()
        columns = []
        for f in range(f0, f0 + count):
            for i in range(4):
                columns.append(jnp.concatenate([got[s, f, 8 * i : 8 * i + 8, :] for s in range(8)], 0))
        wave = from_left(wl_ref[2], jnp.concatenate(columns, 1))
        wave = wave * jnp.concatenate([lam[...]] * count, 1)
        wave = from_left(wl_ref[3], wave)
        for f in range(count):
            for i in range(4):
                n = 4 * f + i
                for s in range(8):
                    back[s, f0 + f, 8 * i : 8 * i + 8, :] = wave[8 * s : 8 * s + 8, 128 * n : 128 * (n + 1)]
        for k in order:
            to = me ^ k
            copy = remote(back.at[to, run], s3.at[run, mine_32], t2_send.at[c, k], t2_recv.at[c, k], peer(to))
            copy.start()
            sent.append(copy)
        s3[f0 : f0 + count, mine_32] = back[me, f0 : f0 + count]

    def give(slot, to, n, device):
        return remote(acc.at[slot], ret.at[to], r_send.at[n], r_recv.at[to], device)

    gives = {
        B: give(B, 1 + h, 0, at(-1, 0)),
        C: give(C, 3, 1, at(-1, h)),
        F: give(F, 4, 2, at(1, h)),
    }
    swap = give(E - h, 0, 3, at(0, 1 - h))
    begun = set()
    left_of = {slot: sum(slot in pair[:2] for pair in PAIRS) for slot in gives}

    def inverse(c):
        f0, count = RUNS[c]
        run = pl.ds(f0, count)
        for k in order:
            remote(
                back.at[0, run], s3.at[run, pl.ds(pl.multiple_of(32 * (me ^ k), 32), 32)],
                t2_send.at[c, k], t2_recv.at[c, k], peer(me ^ k),
            ).wait_recv()
        res = along_y(s3, f0, count, wl_ref[1])
        for n, piece in enumerate(res):
            s4[f0 + n // 8, pl.ds(n % 8, 32, stride=8), :] = piece
        for f in range(f0, f0 + count):
            low, high, _ = PAIRS[f]
            potential = from_right(s4[f], wz_ref[1])
            for j in range(32):
                cut = slice(128 * j, 128 * (j + 1))
                v = potential[8 * j : 8 * j + 8]
                for to, by in ((low, high), (high, low)):
                    term = v * band[by, :, cut]
                    acc[to, :, cut] = acc[to, :, cut] + term if to in begun else term
            begun.update((low, high))
            for slot in (low, high):
                if slot in gives:
                    left_of[slot] -= 1
                    if not left_of[slot]:
                        gives[slot].start()

    steps = {"f": forward, "x": across, "i": inverse}
    for step, c in PLAN:
        steps[step](c)

    def returned(slot):
        give(B, slot, 0, at(-1, 0)).wait_recv()

    returned(4)
    returned(3)
    acc[D] = acc[D] + ret[4]
    acc[E] = acc[E] + ret[3]
    swap.start()

    @pl.when(h == 0)
    def _():
        returned(1)
        returned(2)
        out_ref[0:8, :] = acc[D] + ret[1]
        returned(0)
        out_ref[8:16, :] = ret[0] + ret[2]

    @pl.when(h == 1)
    def _():
        out_ref[8:16, :] = acc[E]
        returned(0)
        out_ref[0:8, :] = ret[0]

    for copy in sent + list(gives.values()) + [swap]:
        copy.wait_send()


def shards(orbitals, counts, partners):
    wz, wl = tables()
    fields = len(PAIRS)
    vmem = pl.BlockSpec(memory_space=pltpu.VMEM)
    hbm = pl.BlockSpec(memory_space=pl.ANY)
    dma = pltpu.SemaphoreType.DMA

    def held(x):
        return pltpu.with_memory_space_constraint(x, pltpu.HBM)

    applied = pl.pallas_call(
        kernel,
        out_shape=jax.ShapeDtypeStruct((16, PLANE), F32),
        in_specs=[hbm] * 5,
        out_specs=vmem,
        scratch_shapes=[
            pltpu.SMEM((1,), jnp.int32),
            pltpu.SMEM((1, 3), jnp.int32),
            pltpu.VMEM(wz.shape, BF16),
            pltpu.VMEM(wl.shape, BF16),
            pltpu.VMEM((5, 8, PLANE), F32),
            pltpu.VMEM((5, 8, 128), F32),
            pltpu.VMEM((fields, 256, 128), F32),
            pltpu.VMEM((fields, 256, 128), F32),
            pltpu.VMEM((8, fields, 32, 128), F32),
            pltpu.VMEM((8, fields, 32, 128), F32),
            pltpu.VMEM((fields, 256, 128), F32),
            pltpu.VMEM((fields, 256, 128), F32),
            pltpu.VMEM((5, 8, PLANE), F32),
            pltpu.VMEM((5, 8, PLANE), F32),
            pltpu.VMEM((NG, 512), F32),
            dma((5,)),
            pltpu.SemaphoreType.REGULAR,
            dma((5,)),
            dma((5,)),
            dma((3,)),
            dma((5,)),
            dma((len(RUNS), 8)),
            dma((len(RUNS), 8)),
            dma((len(RUNS), 8)),
            dma((len(RUNS), 8)),
            dma((4,)),
            dma((5,)),
        ],
        compiler_params=pltpu.CompilerParams(
            collective_id=0, has_side_effects=True, vmem_limit_bytes=24 * 1024 * 1024
        ),
        cost_estimate=pl.CostEstimate(flops=500_000_000, bytes_accessed=1 << 20, transcendentals=0),
    )(held(orbitals.reshape(16, PLANE)), counts, held(partners), held(jnp.asarray(wz)), held(jnp.asarray(wl)))
    return applied.reshape(1, 16, PLANE)


def solution(mesh):
    in_specs = (P("band", "grid", None), P("band"), P("band", None))
    out_specs = P("band", "grid", None)
    return jax.shard_map(shards, mesh=mesh, in_specs=in_specs, out_specs=out_specs, check_vma=False)
```

```python
import functools
import math

import jax
import jax.numpy as jnp
import ml_dtypes
import numpy as np
from jax import lax
from jax.experimental import pallas as pl
from jax.experimental.pallas import tpu as pltpu
from jax.sharding import PartitionSpec as P

MESH = pl.DeviceIdType.MESH
F32, BF16 = jnp.float32, jnp.bfloat16
NG = 64
PLANE = NG * NG
B, C, D, E, F = range(5)
PAIRS = ((D, E, 1), (C, E, 2), (C, D, 1), (C, F, 3), (B, D, 2), (B, E, 3))
RUNS = ((0, 1), (1, 3), (4, 2))
PLAN = (("f", 0), ("f", 1), ("f", 2), ("x", 1), ("x", 2), ("x", 0), ("i", 1), ("i", 2), ("i", 0))


def basis():
    n = np.arange(NG)
    rows = [np.full(NG, 1 / 8)]
    rows += [np.cos(2 * np.pi * k * n / NG) * math.sqrt(2) / 8 for k in range(1, 32)]
    rows += [np.cos(np.pi * n) / 8]
    rows += [np.sin(2 * np.pi * k * n / NG) * math.sqrt(2) / 8 for k in range(1, 32)]
    return np.stack(rows)


def halves(m):
    high = m.astype(np.float32).astype(ml_dtypes.bfloat16)
    low = (m - high.astype(np.float64)).astype(np.float32).astype(ml_dtypes.bfloat16)
    return high, low


def left(m):
    high, low = halves(m)
    return np.concatenate([high, high, low], 1)


def right(m):
    high, low = halves(m)
    return np.concatenate([np.concatenate([high, low], 1), np.concatenate([high, np.zeros_like(low)], 1)], 0)


def tables():
    r = basis()
    zero = np.zeros_like(r)
    z_fwd = np.block([[r.T, zero], [zero, r.T]])
    z_inv = np.block([[r, zero], [zero, r]])
    t = {(e, q): r[32 * e : 32 * e + 32, q::2] for e in range(2) for q in range(2)}
    y_fwd = np.block([[t[0, 0], t[0, 1]], [t[1, 1], t[1, 0]]])
    y_inv = np.block([[t[0, 0].T, t[1, 0].T], [t[1, 1].T, t[0, 1].T]])
    return (
        np.stack([right(z_fwd), right(z_inv)]),
        np.stack([left(y_fwd), left(y_inv), left(r), left(r.T)]),
    )


def split(x):
    high = x.astype(BF16)
    return high, (x - high.astype(F32)).astype(BF16)


def dot(a, b):
    return lax.dot_general(a, b, (((1,), (0,)), ((), ())), preferred_element_type=F32)


def from_left(matrix, x):
    high, low = split(x)
    return dot(matrix, jnp.concatenate([high, low, high], 0))


def from_right(x, matrix):
    high, low = split(x)
    both = dot(jnp.concatenate([high, low], 1), matrix)
    return both[:, :128] + both[:, 128:]


def along_y(ref, first, count, matrix):
    parts = []
    for f in range(first, first + count):
        for x in range(8):
            parts.append(ref[f, pl.ds(x, 32, stride=8), :])
    both = jnp.concatenate(parts, 1)
    other = jnp.concatenate([jnp.concatenate([v[:, 64:], v[:, :64]], 1) for v in parts], 1)
    out = from_left(matrix, jnp.concatenate([both, other], 0))
    lane = lax.broadcasted_iota(jnp.int32, (32, 128), 1)
    res = []
    for n in range(8 * count):
        piece = out[:, 128 * n : 128 * (n + 1)]
        res.append(jnp.where(lane < 64, piece[:32], piece[32:]))
    return res


def freq_sq(index):
    f = jnp.where(index <= 32, index, index - 32).astype(F32) * F32(2 * math.pi / NG)
    return f * f


def kernel(
    orb, counts_in, partners_in, wz_in, wl_in, out_ref,
    counts, partners, wz_ref, wl_ref, band, listed, s1, s2, got, back, s3, s4, acc, ret, lam,
    local_sem, hello, f_send, f_recv, a_send, a_recv, t1_send, t1_recv, t2_send, t2_recv, r_send, r_recv,
):
    m = lax.axis_index("band")
    g = lax.axis_index("grid")
    p, h = m // 2, m % 2
    me = 2 * g + h
    n_bands = 64

    def at(dp, hh):
        return ((2 * p + 2 * dp + n_bands) % n_bands + hh, g)

    def peer(slot):
        return (2 * p + slot % 2, slot // 2)

    def remote(src, dst, send, recv, device):
        return pltpu.make_async_remote_copy(
            src_ref=src, dst_ref=dst, send_sem=send, recv_sem=recv, device_id=device, device_id_type=MESH
        )

    barrier = pltpu.get_barrier_semaphore()
    for device in [at(-1, 0), at(-1, 1)] + [peer(me ^ k) for k in (1, 2, 4, 6)]:
        pl.semaphore_signal(barrier, inc=1, device_id=device, device_id_type=MESH)

    def rows(half):
        return pl.ds(pl.multiple_of(8 * half, 8), 8)

    mine, rest = orb.at[rows(h)], orb.at[rows(1 - h)]
    local = [
        pltpu.make_async_copy(src, dst, local_sem.at[n])
        for n, (src, dst) in enumerate(
            (
                (counts_in, counts), (partners_in, partners), (mine, band.at[D + h]),
                (wz_in, wz_ref), (wl_in, wl_ref),
            )
        )
    ]
    for copy in local:
        copy.start()

    pl.semaphore_wait(barrier, 6)

    def fetch(src, slot, n, device):
        return remote(src, band.at[slot], f_send.at[n], f_recv.at[slot], device)

    def fetched(slot):
        fetch(rest, slot, 0, at(0, 1 - h)).wait_recv()

    def tell(slot, n, device):
        return remote(listed.at[D + h], listed.at[slot], a_send.at[n], a_recv.at[slot], device)

    sent = [
        fetch(rest, D + h, 0, at(0, 1 - h)),
        fetch(mine, B + h, 1, at(1, h)),
    ]
    for copy in sent:
        copy.start()
    for hh in range(2):
        pl.semaphore_signal(hello, inc=1, device_id=at(1, hh), device_id_type=MESH)

    local[0].wait()
    local[1].wait()
    row = lax.broadcasted_iota(jnp.int32, (8, 128), 0)
    tile = jnp.zeros((8, 128), F32)
    for d in range(1, 4):
        weight = jnp.float32(0.0)
        for k in range(3):
            hit = ((partners[0, k] - m + n_bands) % n_bands == d) & (counts[0] > k)
            weight = weight + jnp.where(hit, jnp.float32(1.0), jnp.float32(0.0))
        tile = jnp.where(row == d - 1, weight, tile)
    listed[D + h] = tile
    told = [tell(D + h, 0, at(0, 1 - h)), tell(B + h, 1, at(1, h))]
    for copy in told:
        copy.start()
    sent += told

    kx = freq_sq(lax.broadcasted_iota(jnp.int32, (NG, 128), 0))
    lane = lax.broadcasted_iota(jnp.int32, (NG, 128), 1)
    kz = freq_sq(lane % 64)
    for i in range(4):
        ky = freq_sq(4 * me + i + jnp.where(lane < 64, 0, 32))
        total = kx + ky + kz
        some = total > 0
        lam[:, 128 * i : 128 * (i + 1)] = jnp.where(some, F32(4 * math.pi) / jnp.where(some, total, 1.0), 0.0)

    for copy in local[2:]:
        copy.wait()
    fetched(E - h)
    tell(E - h, 0, at(0, 1 - h)).wait_recv()
    on = [
        fetch(band.at[E - h], C - h, 2, at(1, h)),
        remote(listed.at[E - h], listed.at[C - h], a_send.at[2], a_recv.at[C - h], at(1, h)),
        fetch(band.at[D], F, 3, at(-1, h)),
    ]
    on[0].start()
    on[1].start()
    pl.semaphore_wait(hello, 2)
    on[2].start()
    sent += on
    ready = {D, E}
    order = (1, 3, 5, 7, 4, 6, 2)
    mine_32 = pl.ds(pl.multiple_of(32 * me, 32), 32)

    def forward(c):
        f0, count = RUNS[c]
        run = pl.ds(f0, count)
        for f in range(f0, f0 + count):
            low, high, d = PAIRS[f]
            for slot in (low, high):
                if slot not in ready:
                    fetched(slot)
                    if slot != F:
                        tell(slot, 0, at(0, 1 - h)).wait_recv()
                    ready.add(slot)
            alive = jnp.broadcast_to(listed[low, d - 1 : d, :], (8, 128))
            pieces = []
            for j in range(32):
                cut = slice(128 * j, 128 * (j + 1))
                pieces.append(band[low, :, cut] * band[high, :, cut] * alive)
            s1[f] = from_right(jnp.concatenate(pieces, 0), wz_ref[0])
        res = along_y(s1, f0, count, wl_ref[0])
        for n, piece in enumerate(res):
            s2[f0 + n // 8, pl.ds(n % 8, 32, stride=8), :] = piece
        for k in order:
            to = me ^ k
            copy = remote(
                s2.at[run, pl.ds(pl.multiple_of(32 * to, 32), 32)], got.at[me, run],
                t1_send.at[c, k], t1_recv.at[c, k], peer(to),
            )
            copy.start()
            sent.append(copy)
        got[me, f0 : f0 + count] = s2[f0 : f0 + count, mine_32]

    def across(c):
        f0, count = RUNS[c]
        run = pl.ds(f0, count)
        for k in order:
            remote(
                s2.at[run, pl.ds(0, 32)], got.at[me ^ k, run], t1_send.at[c, k], t1_recv.at[c, k], peer(me ^ k)
            ).wait_recv()
        columns = []
        for f in range(f0, f0 + count):
            for i in range(4):
                columns.append(jnp.concatenate([got[s, f, 8 * i : 8 * i + 8, :] for s in range(8)], 0))
        wave = from_left(wl_ref[2], jnp.concatenate(columns, 1))
        wave = wave * jnp.concatenate([lam[...]] * count, 1)
        wave = from_left(wl_ref[3], wave)
        for f in range(count):
            for i in range(4):
                n = 4 * f + i
                for s in range(8):
                    back[s, f0 + f, 8 * i : 8 * i + 8, :] = wave[8 * s : 8 * s + 8, 128 * n : 128 * (n + 1)]
        for k in order:
            to = me ^ k
            copy = remote(back.at[to, run], s3.at[run, mine_32], t2_send.at[c, k], t2_recv.at[c, k], peer(to))
            copy.start()
            sent.append(copy)
        s3[f0 : f0 + count, mine_32] = back[me, f0 : f0 + count]

    def give(slot, to, n, device):
        return remote(acc.at[slot], ret.at[to], r_send.at[n], r_recv.at[to], device)

    gives = {
        B: give(B, 1, 0, at(-1, h)),
        C: give(C, 3, 1, at(-1, h)),
        F: give(F, 4, 2, at(1, h)),
    }
    swap = give(E - h, 0, 3, at(0, 1 - h))
    begun = set()
    left_of = {slot: sum(slot in pair[:2] for pair in PAIRS) for slot in gives}

    def inverse(c):
        f0, count = RUNS[c]
        run = pl.ds(f0, count)
        for k in order:
            remote(
                back.at[0, run], s3.at[run, pl.ds(pl.multiple_of(32 * (me ^ k), 32), 32)],
                t2_send.at[c, k], t2_recv.at[c, k], peer(me ^ k),
            ).wait_recv()
        res = along_y(s3, f0, count, wl_ref[1])
        for n, piece in enumerate(res):
            s4[f0 + n // 8, pl.ds(n % 8, 32, stride=8), :] = piece
        for f in range(f0, f0 + count):
            low, high, _ = PAIRS[f]
            potential = from_right(s4[f], wz_ref[1])
            for j in range(32):
                cut = slice(128 * j, 128 * (j + 1))
                v = potential[8 * j : 8 * j + 8]
                for to, by in ((low, high), (high, low)):
                    term = v * band[by, :, cut]
                    acc[to, :, cut] = acc[to, :, cut] + term if to in begun else term
            begun.update((low, high))
            for slot in (low, high):
                if slot in gives:
                    left_of[slot] -= 1
                    if not left_of[slot]:
                        gives[slot].start()

    steps = {"f": forward, "x": across, "i": inverse}
    for step, c in PLAN:
        steps[step](c)

    def returned(slot):
        give(B, slot, 0, at(-1, 0)).wait_recv()

    returned(4)
    returned(3)
    returned(1)
    acc[D] = acc[D] + ret[4] + ret[1]
    acc[E] = acc[E] + ret[3]
    swap.start()

    out_ref[rows(h), :] = acc[D + h]
    returned(0)
    out_ref[rows(1 - h), :] = ret[0]

    for copy in sent + list(gives.values()) + [swap]:
        copy.wait_send()


def shards(orbitals, counts, partners):
    wz, wl = tables()
    fields = len(PAIRS)
    vmem = pl.BlockSpec(memory_space=pltpu.VMEM)
    hbm = pl.BlockSpec(memory_space=pl.ANY)
    dma = pltpu.SemaphoreType.DMA

    def held(x):
        return pltpu.with_memory_space_constraint(x, pltpu.HBM)

    applied = pl.pallas_call(
        kernel,
        out_shape=jax.ShapeDtypeStruct((16, PLANE), F32),
        in_specs=[hbm] * 5,
        out_specs=vmem,
        scratch_shapes=[
            pltpu.SMEM((1,), jnp.int32),
            pltpu.SMEM((1, 3), jnp.int32),
            pltpu.VMEM(wz.shape, BF16),
            pltpu.VMEM(wl.shape, BF16),
            pltpu.VMEM((5, 8, PLANE), F32),
            pltpu.VMEM((5, 8, 128), F32),
            pltpu.VMEM((fields, 256, 128), F32),
            pltpu.VMEM((fields, 256, 128), F32),
            pltpu.VMEM((8, fields, 32, 128), F32),
            pltpu.VMEM((8, fields, 32, 128), F32),
            pltpu.VMEM((fields, 256, 128), F32),
            pltpu.VMEM((fields, 256, 128), F32),
            pltpu.VMEM((5, 8, PLANE), F32),
            pltpu.VMEM((5, 8, PLANE), F32),
            pltpu.VMEM((NG, 512), F32),
            dma((5,)),
            pltpu.SemaphoreType.REGULAR,
            dma((5,)),
            dma((5,)),
            dma((3,)),
            dma((5,)),
            dma((len(RUNS), 8)),
            dma((len(RUNS), 8)),
            dma((len(RUNS), 8)),
            dma((len(RUNS), 8)),
            dma((4,)),
            dma((5,)),
        ],
        compiler_params=pltpu.CompilerParams(
            collective_id=0, has_side_effects=True, vmem_limit_bytes=24 * 1024 * 1024
        ),
        cost_estimate=pl.CostEstimate(flops=500_000_000, bytes_accessed=1 << 20, transcendentals=0),
    )(held(orbitals.reshape(16, PLANE)), counts, held(partners), held(jnp.asarray(wz)), held(jnp.asarray(wl)))
    return applied.reshape(1, 16, PLANE)


def solution(mesh):
    in_specs = (P("band", "grid", None), P("band"), P("band", None))
    out_specs = P("band", "grid", None)
    return jax.shard_map(shards, mesh=mesh, in_specs=in_specs, out_specs=out_specs, check_vma=False)
```

```python
import functools
import math

import jax
import jax.numpy as jnp
import ml_dtypes
import numpy as np
from jax import lax
from jax.experimental import pallas as pl
from jax.experimental.pallas import tpu as pltpu
from jax.sharding import PartitionSpec as P

MESH = pl.DeviceIdType.MESH
F32, BF16 = jnp.float32, jnp.bfloat16
NG = 64
PLANE = NG * NG
B, C, D, E, F = range(5)
PAIRS = ((D, E, 1), (C, E, 2), (C, D, 1), (C, F, 3), (B, D, 2), (B, E, 3))
RUNS = ((0, 1), (1, 3), (4, 2))
PLAN = (("f", 0), ("f", 1), ("f", 2), ("x", 1), ("x", 2), ("x", 0), ("i", 1), ("i", 2), ("i", 0))


def basis():
    n = np.arange(NG)
    rows = [np.full(NG, 1 / 8)]
    rows += [np.cos(2 * np.pi * k * n / NG) * math.sqrt(2) / 8 for k in range(1, 32)]
    rows += [np.cos(np.pi * n) / 8]
    rows += [np.sin(2 * np.pi * k * n / NG) * math.sqrt(2) / 8 for k in range(1, 32)]
    return np.stack(rows)


def halves(m):
    high = m.astype(np.float32).astype(ml_dtypes.bfloat16)
    low = (m - high.astype(np.float64)).astype(np.float32).astype(ml_dtypes.bfloat16)
    return high, low


def left(m):
    high, low = halves(m)
    return np.concatenate([high, high, low], 1)


def right(m):
    high, low = halves(m)
    return np.concatenate([np.concatenate([high, low], 1), np.concatenate([high, np.zeros_like(low)], 1)], 0)


def tables():
    r = basis()
    zero = np.zeros_like(r)
    z_fwd = np.block([[r.T, zero], [zero, r.T]])
    z_inv = np.block([[r, zero], [zero, r]])
    t = {(e, q): r[32 * e : 32 * e + 32, q::2] for e in range(2) for q in range(2)}
    y_fwd = np.block([[t[0, 0], t[0, 1]], [t[1, 1], t[1, 0]]])
    y_inv = np.block([[t[0, 0].T, t[1, 0].T], [t[1, 1].T, t[0, 1].T]])
    return (
        np.stack([right(z_fwd), right(z_inv)]),
        np.stack([left(y_fwd), left(y_inv), left(r), left(r.T)]),
    )


def split(x):
    high = x.astype(BF16)
    return high, (x - high.astype(F32)).astype(BF16)


def dot(a, b):
    return lax.dot_general(a, b, (((1,), (0,)), ((), ())), preferred_element_type=F32)


def from_left(matrix, x):
    high, low = split(x)
    return dot(matrix, jnp.concatenate([high, low, high], 0))


def from_right(x, matrix):
    high, low = split(x)
    both = dot(jnp.concatenate([high, low], 1), matrix)
    return both[:, :128] + both[:, 128:]


def along_y(ref, first, count, matrix):
    parts = []
    for f in range(first, first + count):
        for x in range(8):
            parts.append(ref[f, pl.ds(x, 32, stride=8), :])
    both = jnp.concatenate(parts, 1)
    other = jnp.concatenate([jnp.concatenate([v[:, 64:], v[:, :64]], 1) for v in parts], 1)
    out = from_left(matrix, jnp.concatenate([both, other], 0))
    lane = lax.broadcasted_iota(jnp.int32, (32, 128), 1)
    res = []
    for n in range(8 * count):
        piece = out[:, 128 * n : 128 * (n + 1)]
        res.append(jnp.where(lane < 64, piece[:32], piece[32:]))
    return res


def freq_sq(index):
    f = jnp.where(index <= 32, index, index - 32).astype(F32) * F32(2 * math.pi / NG)
    return f * f


def kernel(
    orb, counts_in, partners_in, wz_in, wl_in, out_ref,
    counts, partners, wz_ref, wl_ref, band, listed, s1, s2, got, back, s3, s4, acc, ret, lam,
    local_sem, hello, f_send, f_recv, a_send, a_recv, t1_send, t1_recv, t2_send, t2_recv, r_send, r_recv,
):
    m = lax.axis_index("band")
    g = lax.axis_index("grid")
    p, h = m // 2, m % 2
    me = 2 * g + h
    n_bands = 64

    def at(dp, hh):
        return ((2 * p + 2 * dp + n_bands) % n_bands + hh, g)

    def peer(slot):
        return (2 * p + slot % 2, slot // 2)

    def remote(src, dst, send, recv, device):
        return pltpu.make_async_remote_copy(
            src_ref=src, dst_ref=dst, send_sem=send, recv_sem=recv, device_id=device, device_id_type=MESH
        )

    barrier = pltpu.get_barrier_semaphore()
    for device in [at(-1, 0), at(-1, 1)] + [peer(me ^ k) for k in (1, 2, 4, 6)]:
        pl.semaphore_signal(barrier, inc=1, device_id=device, device_id_type=MESH)

    def rows(half):
        return pl.ds(pl.multiple_of(8 * half, 8), 8)

    mine, rest = orb.at[rows(h)], orb.at[rows(1 - h)]
    local = [
        pltpu.make_async_copy(src, dst, local_sem.at[n])
        for n, (src, dst) in enumerate(
            (
                (counts_in, counts), (partners_in, partners), (mine, band.at[D + h]),
                (wz_in, wz_ref), (wl_in, wl_ref),
            )
        )
    ]
    for copy in local:
        copy.start()

    pl.semaphore_wait(barrier, 6)

    def fetch(src, slot, n, device):
        return remote(src, band.at[slot], f_send.at[n], f_recv.at[slot], device)

    def fetched(slot):
        fetch(rest, slot, 0, at(0, 1 - h)).wait_recv()

    def tell(slot, n, device):
        return remote(listed.at[D + h], listed.at[slot], a_send.at[n], a_recv.at[slot], device)

    sent = [
        fetch(rest, D + h, 0, at(0, 1 - h)),
        fetch(mine, B + h, 1, at(1, h)),
    ]
    for copy in sent:
        copy.start()
    for hh in range(2):
        pl.semaphore_signal(hello, inc=1, device_id=at(1, hh), device_id_type=MESH)

    local[0].wait()
    local[1].wait()
    row = lax.broadcasted_iota(jnp.int32, (8, 128), 0)
    tile = jnp.zeros((8, 128), F32)
    for d in range(1, 4):
        weight = jnp.float32(0.0)
        for k in range(3):
            hit = ((partners[0, k] - m + n_bands) % n_bands == d) & (counts[0] > k)
            weight = weight + jnp.where(hit, jnp.float32(1.0), jnp.float32(0.0))
        tile = jnp.where(row == d - 1, weight, tile)
    listed[D + h] = tile
    told = [tell(D + h, 0, at(0, 1 - h)), tell(B + h, 1, at(1, h))]
    for copy in told:
        copy.start()
    sent += told

    kx = freq_sq(lax.broadcasted_iota(jnp.int32, (NG, 128), 0))
    lane = lax.broadcasted_iota(jnp.int32, (NG, 128), 1)
    kz = freq_sq(lane % 64)
    for i in range(4):
        ky = freq_sq(4 * me + i + jnp.where(lane < 64, 0, 32))
        total = kx + ky + kz
        some = total > 0
        lam[:, 128 * i : 128 * (i + 1)] = jnp.where(some, F32(4 * math.pi) / jnp.where(some, total, 1.0), 0.0)

    for copy in local[2:]:
        copy.wait()
    fetched(E - h)
    tell(E - h, 0, at(0, 1 - h)).wait_recv()
    on = [
        fetch(band.at[E - h], C - h, 2, at(1, h)),
        remote(listed.at[E - h], listed.at[C - h], a_send.at[2], a_recv.at[C - h], at(1, h)),
        fetch(band.at[D], F, 3, at(-1, h)),
    ]
    on[0].start()
    on[1].start()
    pl.semaphore_wait(hello, 2)
    on[2].start()
    sent += on
    ready = {D, E}
    order = (1, 3, 5, 7, 4, 6, 2)
    mine_32 = pl.ds(pl.multiple_of(32 * me, 32), 32)

    def forward(c):
        f0, count = RUNS[c]
        run = pl.ds(f0, count)
        for f in range(f0, f0 + count):
            low, high, d = PAIRS[f]
            for slot in (low, high):
                if slot not in ready:
                    fetched(slot)
                    if slot != F:
                        tell(slot, 0, at(0, 1 - h)).wait_recv()
                    ready.add(slot)
            alive = jnp.broadcast_to(listed[low, d - 1 : d, :], (8, 128))
            pieces = []
            for j in range(32):
                cut = slice(128 * j, 128 * (j + 1))
                pieces.append(band[low, :, cut] * band[high, :, cut] * alive)
            s1[f] = from_right(jnp.concatenate(pieces, 0), wz_ref[0])
        res = along_y(s1, f0, count, wl_ref[0])
        for n, piece in enumerate(res):
            s2[f0 + n // 8, pl.ds(n % 8, 32, stride=8), :] = piece
        for k in order:
            to = me ^ k
            copy = remote(
                s2.at[run, pl.ds(pl.multiple_of(32 * to, 32), 32)], got.at[me, run],
                t1_send.at[c, k], t1_recv.at[c, k], peer(to),
            )
            copy.start()
            sent.append(copy)
        got[me, f0 : f0 + count] = s2[f0 : f0 + count, mine_32]

    def across(c):
        f0, count = RUNS[c]
        run = pl.ds(f0, count)
        for k in order:
            remote(
                s2.at[run, pl.ds(0, 32)], got.at[me ^ k, run], t1_send.at[c, k], t1_recv.at[c, k], peer(me ^ k)
            ).wait_recv()
        columns = []
        for f in range(f0, f0 + count):
            for i in range(4):
                columns.append(jnp.concatenate([got[s, f, 8 * i : 8 * i + 8, :] for s in range(8)], 0))
        wave = from_left(wl_ref[2], jnp.concatenate(columns, 1))
        wave = wave * jnp.concatenate([lam[...]] * count, 1)
        wave = from_left(wl_ref[3], wave)
        for f in range(count):
            for i in range(4):
                n = 4 * f + i
                for s in range(8):
                    back[s, f0 + f, 8 * i : 8 * i + 8, :] = wave[8 * s : 8 * s + 8, 128 * n : 128 * (n + 1)]
        for k in order:
            to = me ^ k
            copy = remote(back.at[to, run], s3.at[run, mine_32], t2_send.at[c, k], t2_recv.at[c, k], peer(to))
            copy.start()
            sent.append(copy)
        s3[f0 : f0 + count, mine_32] = back[me, f0 : f0 + count]

    def give(slot, to, n, device):
        return remote(acc.at[slot], ret.at[to], r_send.at[n], r_recv.at[to], device)

    gives = {
        B: give(B, 1, 0, at(-1, h)),
        C: give(C, 3, 1, at(-1, h)),
        F: give(F, 4, 2, at(1, h)),
    }
    swap = give(E - h, 0, 3, at(0, 1 - h))
    begun = set()
    left_of = {slot: sum(slot in pair[:2] for pair in PAIRS) for slot in gives}

    def inverse(c):
        f0, count = RUNS[c]
        run = pl.ds(f0, count)
        for k in order:
            remote(
                back.at[0, run], s3.at[run, pl.ds(pl.multiple_of(32 * (me ^ k), 32), 32)],
                t2_send.at[c, k], t2_recv.at[c, k], peer(me ^ k),
            ).wait_recv()
        res = along_y(s3, f0, count, wl_ref[1])
        for n, piece in enumerate(res):
            s4[f0 + n // 8, pl.ds(n % 8, 32, stride=8), :] = piece
        for f in range(f0, f0 + count):
            low, high, _ = PAIRS[f]
            potential = from_right(s4[f], wz_ref[1])
            for j in range(32):
                cut = slice(128 * j, 128 * (j + 1))
                v = potential[8 * j : 8 * j + 8]
                for to, by in ((low, high), (high, low)):
                    term = v * band[by, :, cut]
                    acc[to, :, cut] = acc[to, :, cut] + term if to in begun else term
            begun.update((low, high))
            for slot in (low, high):
                if slot in gives:
                    left_of[slot] -= 1
                    if not left_of[slot]:
                        gives[slot].start()

    steps = {"f": forward, "x": across, "i": inverse}
    for step, c in PLAN:
        steps[step](c)

    def returned(slot):
        give(B, slot, 0, at(-1, 0)).wait_recv()

    returned(4)
    returned(3)
    returned(1)
    acc[D] = acc[D] + ret[4] + ret[1]
    acc[E] = acc[E] + ret[3]
    swap.start()

    out_ref[rows(h), :] = acc[D + h]
    for copy in sent + list(gives.values()) + [swap]:
        copy.wait_send()
    returned(0)
    out_ref[rows(1 - h), :] = ret[0]


def shards(orbitals, counts, partners):
    wz, wl = tables()
    fields = len(PAIRS)
    vmem = pl.BlockSpec(memory_space=pltpu.VMEM)
    hbm = pl.BlockSpec(memory_space=pl.ANY)
    dma = pltpu.SemaphoreType.DMA

    def held(x):
        return pltpu.with_memory_space_constraint(x, pltpu.HBM)

    applied = pl.pallas_call(
        kernel,
        out_shape=jax.ShapeDtypeStruct((16, PLANE), F32),
        in_specs=[hbm] * 5,
        out_specs=vmem,
        scratch_shapes=[
            pltpu.SMEM((1,), jnp.int32),
            pltpu.SMEM((1, 3), jnp.int32),
            pltpu.VMEM(wz.shape, BF16),
            pltpu.VMEM(wl.shape, BF16),
            pltpu.VMEM((5, 8, PLANE), F32),
            pltpu.VMEM((5, 8, 128), F32),
            pltpu.VMEM((fields, 256, 128), F32),
            pltpu.VMEM((fields, 256, 128), F32),
            pltpu.VMEM((8, fields, 32, 128), F32),
            pltpu.VMEM((8, fields, 32, 128), F32),
            pltpu.VMEM((fields, 256, 128), F32),
            pltpu.VMEM((fields, 256, 128), F32),
            pltpu.VMEM((5, 8, PLANE), F32),
            pltpu.VMEM((5, 8, PLANE), F32),
            pltpu.VMEM((NG, 512), F32),
            dma((5,)),
            pltpu.SemaphoreType.REGULAR,
            dma((5,)),
            dma((5,)),
            dma((3,)),
            dma((5,)),
            dma((len(RUNS), 8)),
            dma((len(RUNS), 8)),
            dma((len(RUNS), 8)),
            dma((len(RUNS), 8)),
            dma((4,)),
            dma((5,)),
        ],
        compiler_params=pltpu.CompilerParams(
            collective_id=0, has_side_effects=True, vmem_limit_bytes=24 * 1024 * 1024
        ),
        cost_estimate=pl.CostEstimate(flops=500_000_000, bytes_accessed=1 << 20, transcendentals=0),
    )(held(orbitals.reshape(16, PLANE)), counts, held(partners), held(jnp.asarray(wz)), held(jnp.asarray(wl)))
    return applied.reshape(1, 16, PLANE)


def solution(mesh):
    in_specs = (P("band", "grid", None), P("band"), P("band", None))
    out_specs = P("band", "grid", None)
    return jax.shard_map(shards, mesh=mesh, in_specs=in_specs, out_specs=out_specs, check_vma=False)
```

```python
import functools
import math

import jax
import jax.numpy as jnp
import ml_dtypes
import numpy as np
from jax import lax
from jax.experimental import pallas as pl
from jax.experimental.pallas import tpu as pltpu
from jax.sharding import PartitionSpec as P

MESH = pl.DeviceIdType.MESH
F32, BF16 = jnp.float32, jnp.bfloat16
NG = 64
PLANE = NG * NG
B, C, D, E, F = range(5)
PAIRS = ((D, E, 1), (C, E, 2), (C, D, 1), (C, F, 3), (B, D, 2), (B, E, 3))
RUNS = ((0, 1), (1, 3), (4, 2))
PLAN = (("f", 0), ("f", 1), ("f", 2), ("x", 1), ("x", 2), ("x", 0), ("i", 1), ("i", 2), ("i", 0))


def basis():
    n = np.arange(NG)
    rows = [np.full(NG, 1 / 8)]
    rows += [np.cos(2 * np.pi * k * n / NG) * math.sqrt(2) / 8 for k in range(1, 32)]
    rows += [np.cos(np.pi * n) / 8]
    rows += [np.sin(2 * np.pi * k * n / NG) * math.sqrt(2) / 8 for k in range(1, 32)]
    return np.stack(rows)


def halves(m):
    high = m.astype(np.float32).astype(ml_dtypes.bfloat16)
    low = (m - high.astype(np.float64)).astype(np.float32).astype(ml_dtypes.bfloat16)
    return high, low


def left(m):
    high, low = halves(m)
    return np.concatenate([high, high, low], 1)


def right(m):
    high, low = halves(m)
    return np.concatenate([np.concatenate([high, low], 1), np.concatenate([high, np.zeros_like(low)], 1)], 0)


def tables():
    r = basis()
    zero = np.zeros_like(r)
    z_fwd = np.block([[r.T, zero], [zero, r.T]])
    z_inv = np.block([[r, zero], [zero, r]])
    t = {(e, q): r[32 * e : 32 * e + 32, q::2] for e in range(2) for q in range(2)}
    y_fwd = np.block([[t[0, 0], t[0, 1]], [t[1, 1], t[1, 0]]])
    y_inv = np.block([[t[0, 0].T, t[1, 0].T], [t[1, 1].T, t[0, 1].T]])
    return (
        np.stack([right(z_fwd), right(z_inv)]),
        np.stack([left(y_fwd), left(y_inv), left(r), left(r.T)]),
    )


def split(x):
    high = x.astype(BF16)
    return high, (x - high.astype(F32)).astype(BF16)


def dot(a, b):
    return lax.dot_general(a, b, (((1,), (0,)), ((), ())), preferred_element_type=F32)


def from_left(matrix, x):
    high, low = split(x)
    return dot(matrix, jnp.concatenate([high, low, high], 0))


def from_right(x, matrix):
    high, low = split(x)
    both = dot(jnp.concatenate([high, low], 1), matrix)
    return both[:, :128] + both[:, 128:]


def along_y(ref, first, count, matrix):
    parts = []
    for f in range(first, first + count):
        for x in range(8):
            parts.append(ref[f, pl.ds(x, 32, stride=8), :])
    both = jnp.concatenate(parts, 1)
    other = jnp.concatenate([jnp.concatenate([v[:, 64:], v[:, :64]], 1) for v in parts], 1)
    out = from_left(matrix, jnp.concatenate([both, other], 0))
    lane = lax.broadcasted_iota(jnp.int32, (32, 128), 1)
    res = []
    for n in range(8 * count):
        piece = out[:, 128 * n : 128 * (n + 1)]
        res.append(jnp.where(lane < 64, piece[:32], piece[32:]))
    return res


def freq_sq(index):
    f = jnp.where(index <= 32, index, index - 32).astype(F32) * F32(2 * math.pi / NG)
    return f * f


def kernel(
    orb, counts_in, partners_in, wz_in, wl_in, out_ref,
    counts, partners, wz_ref, wl_ref, band, spare, listed, s1, s2, got, back, s3, s4, acc, ret, lam,
    local_sem, hello, f_send, f_recv, a_send, a_recv, t1_send, t1_recv, t2_send, t2_recv, r_send, r_recv,
):
    m = lax.axis_index("band")
    g = lax.axis_index("grid")
    p, h = m // 2, m % 2
    me = 2 * g + h
    n_bands = 64

    def at(dp, hh):
        return ((2 * p + 2 * dp + n_bands) % n_bands + hh, g)

    def peer(slot):
        return (2 * p + slot % 2, slot // 2)

    def remote(src, dst, send, recv, device):
        return pltpu.make_async_remote_copy(
            src_ref=src, dst_ref=dst, send_sem=send, recv_sem=recv, device_id=device, device_id_type=MESH
        )

    barrier = pltpu.get_barrier_semaphore()
    for device in [at(-1, 0), at(-1, 1)] + [peer(me ^ k) for k in (1, 2, 4, 6)]:
        pl.semaphore_signal(barrier, inc=1, device_id=device, device_id_type=MESH)

    def rows(half):
        return pl.ds(pl.multiple_of(8 * half, 8), 8)

    mine, rest = orb.at[rows(h)], orb.at[rows(1 - h)]
    local = [
        pltpu.make_async_copy(src, dst, local_sem.at[n])
        for n, (src, dst) in enumerate(
            (
                (mine, band.at[D + h]), (rest, spare), (counts_in, counts), (partners_in, partners),
                (wz_in, wz_ref), (wl_in, wl_ref),
            )
        )
    ]
    for copy in local:
        copy.start()

    local[1].wait()
    local[0].wait()
    pl.semaphore_wait(barrier, 6)

    def fetch(src, slot, n, device):
        return remote(src, band.at[slot], f_send.at[n], f_recv.at[slot], device)

    def fetched(slot):
        fetch(rest, slot, 0, at(0, 1 - h)).wait_recv()

    def tell(slot, n, device):
        return remote(listed.at[D + h], listed.at[slot], a_send.at[n], a_recv.at[slot], device)

    sent = [
        fetch(spare, D + h, 0, at(0, 1 - h)),
        fetch(band.at[D + h], B + h, 1, at(1, h)),
    ]
    for copy in sent:
        copy.start()
    for hh in range(2):
        pl.semaphore_signal(hello, inc=1, device_id=at(1, hh), device_id_type=MESH)

    local[2].wait()
    local[3].wait()
    row = lax.broadcasted_iota(jnp.int32, (8, 128), 0)
    tile = jnp.zeros((8, 128), F32)
    for d in range(1, 4):
        weight = jnp.float32(0.0)
        for k in range(3):
            hit = ((partners[0, k] - m + n_bands) % n_bands == d) & (counts[0] > k)
            weight = weight + jnp.where(hit, jnp.float32(1.0), jnp.float32(0.0))
        tile = jnp.where(row == d - 1, weight, tile)
    listed[D + h] = tile
    told = [tell(D + h, 0, at(0, 1 - h)), tell(B + h, 1, at(1, h))]
    for copy in told:
        copy.start()
    sent += told

    kx = freq_sq(lax.broadcasted_iota(jnp.int32, (NG, 128), 0))
    lane = lax.broadcasted_iota(jnp.int32, (NG, 128), 1)
    kz = freq_sq(lane % 64)
    for i in range(4):
        ky = freq_sq(4 * me + i + jnp.where(lane < 64, 0, 32))
        total = kx + ky + kz
        some = total > 0
        lam[:, 128 * i : 128 * (i + 1)] = jnp.where(some, F32(4 * math.pi) / jnp.where(some, total, 1.0), 0.0)

    for copy in local[4:]:
        copy.wait()
    fetched(E - h)
    tell(E - h, 0, at(0, 1 - h)).wait_recv()
    on = [
        fetch(band.at[E - h], C - h, 2, at(1, h)),
        remote(listed.at[E - h], listed.at[C - h], a_send.at[2], a_recv.at[C - h], at(1, h)),
        fetch(band.at[D], F, 3, at(-1, h)),
    ]
    on[0].start()
    on[1].start()
    pl.semaphore_wait(hello, 2)
    on[2].start()
    sent += on
    ready = {D, E}
    order = (1, 3, 5, 7, 4, 6, 2)
    mine_32 = pl.ds(pl.multiple_of(32 * me, 32), 32)

    def forward(c):
        f0, count = RUNS[c]
        run = pl.ds(f0, count)
        for f in range(f0, f0 + count):
            low, high, d = PAIRS[f]
            for slot in (low, high):
                if slot not in ready:
                    fetched(slot)
                    if slot != F:
                        tell(slot, 0, at(0, 1 - h)).wait_recv()
                    ready.add(slot)
            alive = jnp.broadcast_to(listed[low, d - 1 : d, :], (8, 128))
            pieces = []
            for j in range(32):
                cut = slice(128 * j, 128 * (j + 1))
                pieces.append(band[low, :, cut] * band[high, :, cut] * alive)
            s1[f] = from_right(jnp.concatenate(pieces, 0), wz_ref[0])
        res = along_y(s1, f0, count, wl_ref[0])
        for n, piece in enumerate(res):
            s2[f0 + n // 8, pl.ds(n % 8, 32, stride=8), :] = piece
        for k in order:
            to = me ^ k
            copy = remote(
                s2.at[run, pl.ds(pl.multiple_of(32 * to, 32), 32)], got.at[me, run],
                t1_send.at[c, k], t1_recv.at[c, k], peer(to),
            )
            copy.start()
            sent.append(copy)
        got[me, f0 : f0 + count] = s2[f0 : f0 + count, mine_32]

    def across(c):
        f0, count = RUNS[c]
        run = pl.ds(f0, count)
        for k in order:
            remote(
                s2.at[run, pl.ds(0, 32)], got.at[me ^ k, run], t1_send.at[c, k], t1_recv.at[c, k], peer(me ^ k)
            ).wait_recv()
        columns = []
        for f in range(f0, f0 + count):
            for i in range(4):
                columns.append(jnp.concatenate([got[s, f, 8 * i : 8 * i + 8, :] for s in range(8)], 0))
        wave = from_left(wl_ref[2], jnp.concatenate(columns, 1))
        wave = wave * jnp.concatenate([lam[...]] * count, 1)
        wave = from_left(wl_ref[3], wave)
        for f in range(count):
            for i in range(4):
                n = 4 * f + i
                for s in range(8):
                    back[s, f0 + f, 8 * i : 8 * i + 8, :] = wave[8 * s : 8 * s + 8, 128 * n : 128 * (n + 1)]
        for k in order:
            to = me ^ k
            copy = remote(back.at[to, run], s3.at[run, mine_32], t2_send.at[c, k], t2_recv.at[c, k], peer(to))
            copy.start()
            sent.append(copy)
        s3[f0 : f0 + count, mine_32] = back[me, f0 : f0 + count]

    def give(slot, to, n, device):
        return remote(acc.at[slot], ret.at[to], r_send.at[n], r_recv.at[to], device)

    gives = {
        B: give(B, 1, 0, at(-1, h)),
        C: give(C, 3, 1, at(-1, h)),
        F: give(F, 4, 2, at(1, h)),
    }
    swap = give(E - h, 0, 3, at(0, 1 - h))
    begun = set()
    left_of = {slot: sum(slot in pair[:2] for pair in PAIRS) for slot in gives}

    def inverse(c):
        f0, count = RUNS[c]
        run = pl.ds(f0, count)
        for k in order:
            remote(
                back.at[0, run], s3.at[run, pl.ds(pl.multiple_of(32 * (me ^ k), 32), 32)],
                t2_send.at[c, k], t2_recv.at[c, k], peer(me ^ k),
            ).wait_recv()
        res = along_y(s3, f0, count, wl_ref[1])
        for n, piece in enumerate(res):
            s4[f0 + n // 8, pl.ds(n % 8, 32, stride=8), :] = piece
        for f in range(f0, f0 + count):
            low, high, _ = PAIRS[f]
            potential = from_right(s4[f], wz_ref[1])
            for j in range(32):
                cut = slice(128 * j, 128 * (j + 1))
                v = potential[8 * j : 8 * j + 8]
                for to, by in ((low, high), (high, low)):
                    term = v * band[by, :, cut]
                    acc[to, :, cut] = acc[to, :, cut] + term if to in begun else term
            begun.update((low, high))
            for slot in (low, high):
                if slot in gives:
                    left_of[slot] -= 1
                    if not left_of[slot]:
                        gives[slot].start()

    steps = {"f": forward, "x": across, "i": inverse}
    for step, c in PLAN:
        steps[step](c)

    def returned(slot):
        give(B, slot, 0, at(-1, 0)).wait_recv()

    returned(4)
    returned(3)
    returned(1)
    acc[D] = acc[D] + ret[4] + ret[1]
    acc[E] = acc[E] + ret[3]
    swap.start()

    out_ref[rows(h), :] = acc[D + h]
    for copy in sent + list(gives.values()) + [swap]:
        copy.wait_send()
    returned(0)
    out_ref[rows(1 - h), :] = ret[0]


def shards(orbitals, counts, partners):
    wz, wl = tables()
    fields = len(PAIRS)
    vmem = pl.BlockSpec(memory_space=pltpu.VMEM)
    hbm = pl.BlockSpec(memory_space=pl.ANY)
    dma = pltpu.SemaphoreType.DMA

    def held(x):
        return pltpu.with_memory_space_constraint(x, pltpu.HBM)

    applied = pl.pallas_call(
        kernel,
        out_shape=jax.ShapeDtypeStruct((16, PLANE), F32),
        in_specs=[hbm] * 5,
        out_specs=vmem,
        scratch_shapes=[
            pltpu.SMEM((1,), jnp.int32),
            pltpu.SMEM((1, 3), jnp.int32),
            pltpu.VMEM(wz.shape, BF16),
            pltpu.VMEM(wl.shape, BF16),
            pltpu.VMEM((5, 8, PLANE), F32),
            pltpu.VMEM((8, PLANE), F32),
            pltpu.VMEM((5, 8, 128), F32),
            pltpu.VMEM((fields, 256, 128), F32),
            pltpu.VMEM((fields, 256, 128), F32),
            pltpu.VMEM((8, fields, 32, 128), F32),
            pltpu.VMEM((8, fields, 32, 128), F32),
            pltpu.VMEM((fields, 256, 128), F32),
            pltpu.VMEM((fields, 256, 128), F32),
            pltpu.VMEM((5, 8, PLANE), F32),
            pltpu.VMEM((5, 8, PLANE), F32),
            pltpu.VMEM((NG, 512), F32),
            dma((6,)),
            pltpu.SemaphoreType.REGULAR,
            dma((5,)),
            dma((5,)),
            dma((3,)),
            dma((5,)),
            dma((len(RUNS), 8)),
            dma((len(RUNS), 8)),
            dma((len(RUNS), 8)),
            dma((len(RUNS), 8)),
            dma((4,)),
            dma((5,)),
        ],
        compiler_params=pltpu.CompilerParams(
            collective_id=0, has_side_effects=True, vmem_limit_bytes=24 * 1024 * 1024
        ),
        cost_estimate=pl.CostEstimate(flops=500_000_000, bytes_accessed=1 << 20, transcendentals=0),
    )(held(orbitals.reshape(16, PLANE)), counts, held(partners), held(jnp.asarray(wz)), held(jnp.asarray(wl)))
    return applied.reshape(1, 16, PLANE)


def solution(mesh):
    in_specs = (P("band", "grid", None), P("band"), P("band", None))
    out_specs = P("band", "grid", None)
    return jax.shard_map(shards, mesh=mesh, in_specs=in_specs, out_specs=out_specs, check_vma=False)
```

```python
import functools
import math

import jax
import jax.numpy as jnp
import ml_dtypes
import numpy as np
from jax import lax
from jax.experimental import pallas as pl
from jax.experimental.pallas import tpu as pltpu
from jax.sharding import PartitionSpec as P

MESH = pl.DeviceIdType.MESH
F32, BF16 = jnp.float32, jnp.bfloat16
NG = 64
PLANE = NG * NG
B, C, D, E, F = range(5)
PAIRS = ((D, E, 1), (C, E, 2), (C, D, 1), (C, F, 3), (B, D, 2), (B, E, 3))
RUNS = ((0, 1), (1, 3), (4, 2))
PLAN = (("f", 0), ("f", 1), ("f", 2), ("x", 1), ("x", 2), ("x", 0), ("i", 1), ("i", 2), ("i", 0))


def basis():
    n = np.arange(NG)
    rows = [np.full(NG, 1 / 8)]
    rows += [np.cos(2 * np.pi * k * n / NG) * math.sqrt(2) / 8 for k in range(1, 32)]
    rows += [np.cos(np.pi * n) / 8]
    rows += [np.sin(2 * np.pi * k * n / NG) * math.sqrt(2) / 8 for k in range(1, 32)]
    return np.stack(rows)


def halves(m):
    high = m.astype(np.float32).astype(ml_dtypes.bfloat16)
    low = (m - high.astype(np.float64)).astype(np.float32).astype(ml_dtypes.bfloat16)
    return high, low


def left(m):
    high, low = halves(m)
    return np.concatenate([high, high, low], 1)


def right(m):
    high, low = halves(m)
    return np.concatenate([np.concatenate([high, low], 1), np.concatenate([high, np.zeros_like(low)], 1)], 0)


def tables():
    r = basis()
    zero = np.zeros_like(r)
    z_fwd = np.block([[r.T, zero], [zero, r.T]])
    z_inv = np.block([[r, zero], [zero, r]])
    t = {(e, q): r[32 * e : 32 * e + 32, q::2] for e in range(2) for q in range(2)}
    y_fwd = np.block([[t[0, 0], t[0, 1]], [t[1, 1], t[1, 0]]])
    y_inv = np.block([[t[0, 0].T, t[1, 0].T], [t[1, 1].T, t[0, 1].T]])
    return (
        np.stack([right(z_fwd), right(z_inv)]),
        np.stack([left(y_fwd), left(y_inv), left(r), left(r.T)]),
    )


def split(x):
    high = x.astype(BF16)
    return high, (x - high.astype(F32)).astype(BF16)


def dot(a, b):
    return lax.dot_general(a, b, (((1,), (0,)), ((), ())), preferred_element_type=F32)


def from_left(matrix, x):
    high, low = split(x)
    return dot(matrix, jnp.concatenate([high, low, high], 0))


def from_right(x, matrix):
    high, low = split(x)
    both = dot(jnp.concatenate([high, low], 1), matrix)
    return both[:, :128] + both[:, 128:]


def along_y(ref, first, count, matrix):
    parts = []
    for f in range(first, first + count):
        for x in range(8):
            parts.append(ref[f, pl.ds(x, 32, stride=8), :])
    both = jnp.concatenate(parts, 1)
    other = jnp.concatenate([jnp.concatenate([v[:, 64:], v[:, :64]], 1) for v in parts], 1)
    out = from_left(matrix, jnp.concatenate([both, other], 0))
    lane = lax.broadcasted_iota(jnp.int32, (32, 128), 1)
    res = []
    for n in range(8 * count):
        piece = out[:, 128 * n : 128 * (n + 1)]
        res.append(jnp.where(lane < 64, piece[:32], piece[32:]))
    return res


def freq_sq(index):
    f = jnp.where(index <= 32, index, index - 32).astype(F32) * F32(2 * math.pi / NG)
    return f * f


def kernel(
    orb, counts_in, partners_in, wz_in, wl_in, out_ref,
    counts, partners, wz_ref, wl_ref, band, spare, listed, s1, s2, got, back, s3, s4, acc, ret, lam,
    local_sem, hello, f_send, f_recv, a_send, a_recv, t1_send, t1_recv, t2_send, t2_recv, r_send, r_recv,
):
    m = lax.axis_index("band")
    g = lax.axis_index("grid")
    p, h = m // 2, m % 2
    me = 2 * g + h
    n_bands = 64

    def at(dp, hh):
        return ((2 * p + 2 * dp + n_bands) % n_bands + hh, g)

    def peer(slot):
        return (2 * p + slot % 2, slot // 2)

    def remote(src, dst, send, recv, device):
        return pltpu.make_async_remote_copy(
            src_ref=src, dst_ref=dst, send_sem=send, recv_sem=recv, device_id=device, device_id_type=MESH
        )

    barrier = pltpu.get_barrier_semaphore()
    for device in [at(-1, 0), at(-1, 1)] + [peer(me ^ k) for k in (1, 2, 4, 6)]:
        pl.semaphore_signal(barrier, inc=1, device_id=device, device_id_type=MESH)

    def rows(half):
        return pl.ds(pl.multiple_of(8 * half, 8), 8)

    mine, rest = orb.at[rows(h)], orb.at[rows(1 - h)]
    local = [
        pltpu.make_async_copy(src, dst, local_sem.at[n])
        for n, (src, dst) in enumerate(
            (
                (mine, band.at[D + h]), (rest, spare), (counts_in, counts), (partners_in, partners),
                (wz_in, wz_ref), (wl_in, wl_ref),
            )
        )
    ]
    for copy in local:
        copy.start()

    local[1].wait()
    local[0].wait()
    pl.semaphore_wait(barrier, 6)

    def fetch(src, slot, n, device):
        return remote(src, band.at[slot], f_send.at[n], f_recv.at[slot], device)

    def fetched(slot):
        fetch(rest, slot, 0, at(0, 1 - h)).wait_recv()

    def tell(slot, n, device):
        return remote(listed.at[D + h], listed.at[slot], a_send.at[n], a_recv.at[slot], device)

    sent = [
        fetch(spare, D + h, 0, at(0, 1 - h)),
        fetch(band.at[D + h], B + h, 1, at(1, h)),
    ]
    for copy in sent:
        copy.start()
    for hh in range(2):
        pl.semaphore_signal(hello, inc=1, device_id=at(1, hh), device_id_type=MESH)

    local[2].wait()
    local[3].wait()
    row = lax.broadcasted_iota(jnp.int32, (8, 128), 0)
    tile = jnp.zeros((8, 128), F32)
    for d in range(1, 4):
        weight = jnp.float32(0.0)
        for k in range(3):
            hit = ((partners[0, k] - m + n_bands) % n_bands == d) & (counts[0] > k)
            weight = weight + jnp.where(hit, jnp.float32(1.0), jnp.float32(0.0))
        tile = jnp.where(row == d - 1, weight, tile)
    listed[D + h] = tile
    told = [tell(D + h, 0, at(0, 1 - h)), tell(B + h, 1, at(1, h))]
    for copy in told:
        copy.start()
    sent += told

    kx = freq_sq(lax.broadcasted_iota(jnp.int32, (NG, 128), 0))
    lane = lax.broadcasted_iota(jnp.int32, (NG, 128), 1)
    kz = freq_sq(lane % 64)
    for i in range(4):
        ky = freq_sq(4 * me + i + jnp.where(lane < 64, 0, 32))
        total = kx + ky + kz
        some = total > 0
        lam[:, 128 * i : 128 * (i + 1)] = jnp.where(some, F32(4 * math.pi) / jnp.where(some, total, 1.0), 0.0)

    for copy in local[4:]:
        copy.wait()
    fetched(E - h)
    tell(E - h, 0, at(0, 1 - h)).wait_recv()
    on = [
        fetch(band.at[E - h], C - h, 2, at(1, h)),
        remote(listed.at[E - h], listed.at[C - h], a_send.at[2], a_recv.at[C - h], at(1, h)),
        fetch(band.at[D], F, 3, at(-1, h)),
    ]
    on[0].start()
    on[1].start()
    pl.semaphore_wait(hello, 2)
    on[2].start()
    sent += on
    ready = {D, E}
    order = (1, 3, 5, 7, 4, 6, 2)
    mine_32 = pl.ds(pl.multiple_of(32 * me, 32), 32)

    def forward(c):
        f0, count = RUNS[c]
        run = pl.ds(f0, count)
        for f in range(f0, f0 + count):
            low, high, d = PAIRS[f]
            for slot in (low, high):
                if slot not in ready:
                    fetched(slot)
                    if slot != F:
                        tell(slot, 0, at(0, 1 - h)).wait_recv()
                    ready.add(slot)
            alive = jnp.broadcast_to(listed[low, d - 1 : d, :], (8, 128))
            pieces = []
            for j in range(32):
                cut = slice(128 * j, 128 * (j + 1))
                pieces.append(band[low, :, cut] * band[high, :, cut] * alive)
            s1[f] = from_right(jnp.concatenate(pieces, 0), wz_ref[0])
        res = along_y(s1, f0, count, wl_ref[0])
        for n, piece in enumerate(res):
            s2[f0 + n // 8, pl.ds(n % 8, 32, stride=8), :] = piece
        for k in order:
            to = me ^ k
            copy = remote(
                s2.at[run, pl.ds(pl.multiple_of(32 * to, 32), 32)], got.at[me, run],
                t1_send.at[c, k], t1_recv.at[c, k], peer(to),
            )
            copy.start()
            sent.append(copy)
        got[me, f0 : f0 + count] = s2[f0 : f0 + count, mine_32]

    def across(c):
        f0, count = RUNS[c]
        run = pl.ds(f0, count)
        for k in order:
            remote(
                s2.at[run, pl.ds(0, 32)], got.at[me ^ k, run], t1_send.at[c, k], t1_recv.at[c, k], peer(me ^ k)
            ).wait_recv()
        columns = []
        for f in range(f0, f0 + count):
            for i in range(4):
                columns.append(jnp.concatenate([got[s, f, 8 * i : 8 * i + 8, :] for s in range(8)], 0))
        wave = from_left(wl_ref[2], jnp.concatenate(columns, 1))
        wave = wave * jnp.concatenate([lam[...]] * count, 1)
        wave = from_left(wl_ref[3], wave)
        for f in range(count):
            for i in range(4):
                n = 4 * f + i
                for s in range(8):
                    back[s, f0 + f, 8 * i : 8 * i + 8, :] = wave[8 * s : 8 * s + 8, 128 * n : 128 * (n + 1)]
        for k in order:
            to = me ^ k
            copy = remote(back.at[to, run], s3.at[run, mine_32], t2_send.at[c, k], t2_recv.at[c, k], peer(to))
            copy.start()
            sent.append(copy)
        s3[f0 : f0 + count, mine_32] = back[me, f0 : f0 + count]

    def give(slot, to, n, device):
        return remote(acc.at[slot], ret.at[to], r_send.at[n], r_recv.at[to], device)

    gives = {
        B: give(B, 1, 0, at(-1, h)),
        C: give(C, 3, 1, at(-1, h)),
        F: give(F, 4, 2, at(1, h)),
    }
    swap = give(E - h, 0, 3, at(0, 1 - h))
    begun = set()
    left_of = {slot: sum(slot in pair[:2] for pair in PAIRS) for slot in gives}

    def inverse(c):
        f0, count = RUNS[c]
        run = pl.ds(f0, count)
        for k in order:
            remote(
                back.at[0, run], s3.at[run, pl.ds(pl.multiple_of(32 * (me ^ k), 32), 32)],
                t2_send.at[c, k], t2_recv.at[c, k], peer(me ^ k),
            ).wait_recv()
        res = along_y(s3, f0, count, wl_ref[1])
        for n, piece in enumerate(res):
            s4[f0 + n // 8, pl.ds(n % 8, 32, stride=8), :] = piece
        for f in range(f0, f0 + count):
            low, high, _ = PAIRS[f]
            potential = from_right(s4[f], wz_ref[1])
            for j in range(32):
                cut = slice(128 * j, 128 * (j + 1))
                v = potential[8 * j : 8 * j + 8]
                for to, by in ((low, high), (high, low)):
                    term = v * band[by, :, cut]
                    acc[to, :, cut] = acc[to, :, cut] + term if to in begun else term
            begun.update((low, high))
            for slot in (low, high):
                if slot in gives:
                    left_of[slot] -= 1
                    if not left_of[slot]:
                        gives[slot].start()

    steps = {"f": forward, "x": across, "i": inverse}
    for step, c in PLAN:
        steps[step](c)

    def returned(slot):
        give(B, slot, 0, at(-1, 0)).wait_recv()

    returned(4)
    acc[D] = acc[D] + ret[4]
    returned(3)
    acc[E] = acc[E] + ret[3]
    returned(1)
    acc[D] = acc[D] + ret[1]
    swap.start()

    out_ref[rows(h), :] = acc[D + h]
    for copy in sent + list(gives.values()) + [swap]:
        copy.wait_send()
    returned(0)
    out_ref[rows(1 - h), :] = ret[0]


def shards(orbitals, counts, partners):
    wz, wl = tables()
    fields = len(PAIRS)
    vmem = pl.BlockSpec(memory_space=pltpu.VMEM)
    hbm = pl.BlockSpec(memory_space=pl.ANY)
    dma = pltpu.SemaphoreType.DMA

    def held(x):
        return pltpu.with_memory_space_constraint(x, pltpu.HBM)

    applied = pl.pallas_call(
        kernel,
        out_shape=jax.ShapeDtypeStruct((16, PLANE), F32),
        in_specs=[hbm] * 5,
        out_specs=vmem,
        scratch_shapes=[
            pltpu.SMEM((1,), jnp.int32),
            pltpu.SMEM((1, 3), jnp.int32),
            pltpu.VMEM(wz.shape, BF16),
            pltpu.VMEM(wl.shape, BF16),
            pltpu.VMEM((5, 8, PLANE), F32),
            pltpu.VMEM((8, PLANE), F32),
            pltpu.VMEM((5, 8, 128), F32),
            pltpu.VMEM((fields, 256, 128), F32),
            pltpu.VMEM((fields, 256, 128), F32),
            pltpu.VMEM((8, fields, 32, 128), F32),
            pltpu.VMEM((8, fields, 32, 128), F32),
            pltpu.VMEM((fields, 256, 128), F32),
            pltpu.VMEM((fields, 256, 128), F32),
            pltpu.VMEM((5, 8, PLANE), F32),
            pltpu.VMEM((5, 8, PLANE), F32),
            pltpu.VMEM((NG, 512), F32),
            dma((6,)),
            pltpu.SemaphoreType.REGULAR,
            dma((5,)),
            dma((5,)),
            dma((3,)),
            dma((5,)),
            dma((len(RUNS), 8)),
            dma((len(RUNS), 8)),
            dma((len(RUNS), 8)),
            dma((len(RUNS), 8)),
            dma((4,)),
            dma((5,)),
        ],
        compiler_params=pltpu.CompilerParams(
            collective_id=0, has_side_effects=True, vmem_limit_bytes=24 * 1024 * 1024
        ),
        cost_estimate=pl.CostEstimate(flops=500_000_000, bytes_accessed=1 << 20, transcendentals=0),
    )(held(orbitals.reshape(16, PLANE)), counts, held(partners), held(jnp.asarray(wz)), held(jnp.asarray(wl)))
    return applied.reshape(1, 16, PLANE)


def solution(mesh):
    in_specs = (P("band", "grid", None), P("band"), P("band", None))
    out_specs = P("band", "grid", None)
    return jax.shard_map(shards, mesh=mesh, in_specs=in_specs, out_specs=out_specs, check_vma=False)
```
